32 devices in a mesh: wide: 8 (over z, y), narrow: 4 (over x, core).
Axes of the slice: x: 2, y: 2, z: 4, core: 2. Of those that a mesh axis runs over, the one named last changes fastest.
Arguments:
- queries: bfloat16 [4096, 2048], P(('wide', 'narrow')), may hold values from -8 to 8
- key_tensor: bfloat16 [4096, 256], P(('wide', 'narrow')), may hold values from -8 to 8
- value_tensor: bfloat16 [4096, 256], P(('wide', 'narrow')), may hold values from -8 to 8
- decay_logarithm: float32 [2, 4096], P(None, ('wide', 'narrow')), may hold values from -2 to 0
- lin_gain: float32 [2048], replicated, may hold values from 0.25 to 1.75
- routes: int32 [4096, 2], P(('wide', 'narrow')), may hold values from 0 to 31, all different within a row; in each aligned block of 128 rows (0 to 127, 128 to 255, ...) at most 12 rows name the same one
- route_weight: float32 [4096, 2], P(('wide', 'narrow')), may hold values from 0.2 to 1
- w_up: bfloat16 [2048, 45056], P(None, 'wide'), may hold values from -0.125 to 0.125
- w_down: bfloat16 [45056, 2048], P('wide'), may hold values from -0.15625 to 0.15625
Outputs:
- layer_out: bfloat16 [4096, 2048], P(('wide', 'narrow'))
The draws below stay inside these ranges and needn't reach their ends.
Inputs may be any that keep to these rules, and one draw needn't show every extreme that they name: `routes`: each row names 2 different experts. In each aligned block of 128 rows no expert is named more than 12 times, and in some block some expert is named exactly 12 times.
All inputs are finite; a program needn't handle non-finite values.
Results may differ from the reference program's by a relative error of at most 0.0055.
Values may be sent and summed in bfloat16 or wider, within the bound.
A program may use at most 128 MiB of HBM per device.

```python
import math
import jax
import jax.numpy as jnp
import numpy as np
from jax import lax

MODEL_SPAN = 2048
QUERY_HEADS = 16
PAIRED_KV_PARTS = 2
HEAD_SIZE = 128
FF = 1408
EXPERTS = 32
TOP = 2
QUART = 4
WINDOW_KEYS = 128
DEVICE_TOKENS = 128
MOST = 12
SEGMENT_ITEMS = 4096
N_WIDE = 8
N_NARROW = 4


def attention_inputs(key):
    stochastic_seeds = jax.random.split(jax.random.fold_in(key, 23), 2)
    query_vals = jnp.clip(jax.random.normal(stochastic_seeds[0], (SEGMENT_ITEMS, MODEL_SPAN), jnp.float32), -8.0, 8.0)
    key_entries = jnp.clip(jax.random.normal(stochastic_seeds[1], (SEGMENT_ITEMS, PAIRED_KV_PARTS * HEAD_SIZE), jnp.float32), -8.0, 8.0)
    return (query_vals, key_entries)


def draw_queries(key, part):
    return attention_inputs(key)[0].astype(jnp.bfloat16)


def draw_key_tensor(key, part):
    return attention_inputs(key)[1].astype(jnp.bfloat16)


def draw_value_tensor(key, part):
    stochastic_seeds = jax.random.split(jax.random.fold_in(key, 37), 1)
    random_noise = jax.random.normal(stochastic_seeds[0], (SEGMENT_ITEMS, PAIRED_KV_PARTS * HEAD_SIZE), jnp.float32)
    return jnp.clip(random_noise, -8.0, 8.0).astype(jnp.bfloat16)


def draw_decay_logarithm(key, part):
    stochastic_seeds = jax.random.split(jax.random.fold_in(key, 11), 8)
    block_number = SEGMENT_ITEMS // DEVICE_TOKENS
    quick_count = jax.random.randint(stochastic_seeds[0], (), 1, PAIRED_KV_PARTS)
    rank_order = jax.random.permutation(stochastic_seeds[1], PAIRED_KV_PARTS)
    quick_flag = rank_order < quick_count
    gentle_rate = jnp.exp(jax.random.uniform(stochastic_seeds[2], (PAIRED_KV_PARTS,), jnp.float32, math.log(0.2), math.log(0.6))) / SEGMENT_ITEMS
    quick_rate = jnp.exp(jax.random.uniform(stochastic_seeds[3], (PAIRED_KV_PARTS,), jnp.float32, math.log(0.75), math.log(1.33))) / min(40, DEVICE_TOKENS // 2)
    base_rate = jnp.where(quick_flag, quick_rate, gentle_rate)
    block_multiplier = jnp.exp(jax.random.uniform(stochastic_seeds[4], (PAIRED_KV_PARTS, block_number), jnp.float32, math.log(0.5), math.log(2.0)))
    block_multiplier = jnp.repeat(block_multiplier, DEVICE_TOKENS, axis=1)
    coarseness = jax.random.uniform(stochastic_seeds[5], (PAIRED_KV_PARTS, SEGMENT_ITEMS), jnp.float32, 0.5, 1.5)
    fading_coefficient = -base_rate[:, None] * block_multiplier * coarseness
    spike_location = jax.random.randint(stochastic_seeds[6], (PAIRED_KV_PARTS, 2), 0, SEGMENT_ITEMS)
    spike_persistence = jax.random.uniform(stochastic_seeds[7], (PAIRED_KV_PARTS, 2), jnp.float32, 0.5, 0.8)
    equality_markers = (jnp.arange(SEGMENT_ITEMS)[None, None, :] == spike_location[:, :, None]).astype(jnp.float32)
    fading_coefficient = fading_coefficient + jnp.sum(equality_markers * jnp.log(spike_persistence)[:, :, None], axis=1)
    return fading_coefficient.astype(jnp.float32)


def levels(rng, dims, cuts, least, high):
    level = 1.0
    for axis_at, blocks in cuts:
        steps = jax.random.uniform(jax.random.fold_in(jax.random.fold_in(rng, 6), axis_at), (blocks,), jnp.float32, least / len(cuts), high / len(cuts))
        level = level * jnp.repeat(jnp.exp(steps), dims[axis_at] // blocks).reshape((-1,) + (1,) * (len(dims) - 1 - axis_at))
    return level


def assign_block(stream_key, own, number, rows, count, top, most, skew):
    sequence = jax.random.permutation(stream_key, count)
    heavy_load, ordinary = load_shares(count, rows * top, most, skew, True), load_shares(count, rows * top, most, skew, False)
    places = jnp.arange(count)

    def named(tallies, offset_by):
        used = int((tallies > 0).sum())
        fixed = max(1, used // 4)
        moved = fixed + (places - fixed + offset_by * (used - fixed)) % max(1, count - fixed)
        return jnp.zeros((count,), jnp.int32).at[sequence[jnp.where(places < fixed, places, moved)]].set(jnp.asarray(tallies, jnp.int32))

    tallies = jnp.where(number % 4 == 0, named(heavy_load, number // 4), named(ordinary, number - number // 4 - 1))
    mixed = jax.random.permutation(jax.random.fold_in(own, 3), count)
    giver, taker = mixed[0:count // 2 * 2:2], mixed[1:count // 2 * 2:2]
    slack = jnp.minimum(tallies[giver] - 1, most - tallies[taker]) // 2
    slack = jnp.where((giver == sequence[0]) | (taker == sequence[0]) | (tallies[taker] == 0), 0, jnp.maximum(slack, 0))
    moved = jax.random.randint(jax.random.fold_in(own, 4), (count // 2,), 0, 1 << 20) % (slack + 1)
    tallies = tallies.at[giver].add(-moved).at[taker].add(moved)
    items = jnp.searchsorted(jnp.cumsum(tallies), jnp.arange(rows * top), side="right").astype(jnp.int32)
    table = items.reshape(top, rows).T
    table = table[jax.random.permutation(jax.random.fold_in(own, 1), rows)]
    offset_by = jax.random.randint(jax.random.fold_in(own, 2), (rows, 1), 0, top)
    return jnp.take_along_axis(table, (jnp.arange(top)[None, :] + offset_by) % top, axis=1)


def load_shares(number_of, total, reach, slope, full):
    portions = [(1 << 20) // math.isqrt(standing ** slope) + 1 for standing in range(1, number_of + 1)]
    largest = reach if full else min(reach, max(-(-total // number_of), total * portions[0] // sum(portions)))
    least = 1 if total - largest >= number_of - 1 else 0
    counts, surplus = [largest] + [least] * (number_of - 1), total - largest - least * (number_of - 1)
    while surplus > 0:
        candidates = [i for i in range(1, number_of) if counts[i] < largest] or [i for i in range(1, number_of) if counts[i] < reach]
        whole, left = sum([portions[i] for i in candidates]), surplus
        for i in candidates:
            more = min(reach - counts[i], max(1, left * portions[i] // whole), surplus)
            counts[i] = counts[i] + more
            surplus = surplus - more
    return np.array(counts)


def gaussian(key, extent, deviation, most, cuts=(), held_as=jnp.bfloat16):
    values = jax.random.normal(key, extent, jnp.float32) * deviation
    if len(cuts) > 0:
        values = levels(key, extent, cuts, -0.22, 0.18) * values
    return jnp.clip(values, min=-most, max=most).astype(held_as)


def setup_inputs(seed: int = 0) -> dict:
    keys = jax.random.split(jax.random.key(seed), 10)
    queries = draw_queries(jax.random.fold_in(keys[9], 71), 0)
    key_tensor = draw_key_tensor(jax.random.fold_in(keys[9], 71), 0)
    value_tensor = draw_value_tensor(jax.random.fold_in(keys[9], 71), 0)
    decay_logarithm = draw_decay_logarithm(jax.random.fold_in(keys[9], 71), 0)
    lin_gain = jnp.clip(1.0 + 0.15 * jax.random.normal(keys[4], (MODEL_SPAN,), jnp.float32), 0.25, 1.75)
    routes_keys = jax.random.split(jax.random.fold_in(keys[5], 1), SEGMENT_ITEMS // DEVICE_TOKENS)
    routes_turns = jax.random.permutation(jax.random.fold_in(keys[5], 3), SEGMENT_ITEMS // DEVICE_TOKENS)
    routes = jax.vmap(lambda own, number: assign_block(jax.random.fold_in(keys[5], 2), own, number, DEVICE_TOKENS, EXPERTS, TOP, MOST, 2))(routes_keys, routes_turns).reshape((SEGMENT_ITEMS, TOP))
    route_weight = jnp.clip(0.2 + 0.8 * jax.random.uniform(keys[6], (SEGMENT_ITEMS, TOP), jnp.float32) ** levels(keys[6], (SEGMENT_ITEMS, TOP), ((0, 32),), -0.2, 0.2), 0.2, 1.0)
    w_up = gaussian(keys[7], (MODEL_SPAN, EXPERTS * FF), MODEL_SPAN ** -0.5, 0.125, ((1, 8),))
    w_down = gaussian(keys[8], (EXPERTS * FF, MODEL_SPAN), FF ** -0.5, 0.15625, ((0, 8),))
    return dict(queries=queries, key_tensor=key_tensor, value_tensor=value_tensor, decay_logarithm=decay_logarithm, lin_gain=lin_gain, routes=routes, route_weight=route_weight, w_up=w_up, w_down=w_down)


def reference(queries, key_tensor, value_tensor, decay_logarithm, lin_gain, routes, route_weight, w_up, w_down):
    group_extent = QUERY_HEADS // PAIRED_KV_PARTS
    block_length = min(512, SEGMENT_ITEMS)
    block_number = SEGMENT_ITEMS // block_length
    hi_prec = lax.Precision.HIGHEST
    scale_multiplier = HEAD_SIZE ** (-0.5)
    query_single = queries.astype(jnp.float32).reshape(block_number, block_length, PAIRED_KV_PARTS, group_extent, HEAD_SIZE)
    key_single = key_tensor.astype(jnp.float32).reshape(block_number, block_length, PAIRED_KV_PARTS, HEAD_SIZE) * scale_multiplier
    value_single = value_tensor.astype(jnp.float32).reshape(block_number, block_length, PAIRED_KV_PARTS, HEAD_SIZE)
    blocked_decay = jnp.transpose(decay_logarithm.reshape(PAIRED_KV_PARTS, block_number, block_length), (1, 0, 2))
    position = jnp.arange(block_length)
    causal = position[:, None] >= position[None, :]

    def linear_block(state, inputs):
        query_bfloat, key_bfloat, value_bfloat, decay_b = inputs
        cum_decay = jnp.cumsum(decay_b, axis=1)
        end_decay = cum_decay[:, -1]
        gap_decay = cum_decay[:, :, None] - cum_decay[:, None, :]
        weight_mask = jnp.where(causal[None], jnp.exp(jnp.where(causal[None], gap_decay, 0.0)), 0.0)
        inner_scores = jnp.einsum('thgd,shd->hgts', query_bfloat, key_bfloat, precision=hi_prec) * weight_mask[:, None]
        inner_out = jnp.einsum('hgts,shd->thgd', inner_scores, value_bfloat, precision=hi_prec)
        carried = jnp.einsum('thgd,hde->thge', query_bfloat, state, precision=hi_prec) * jnp.exp(cum_decay).T[:, :, None, None]
        tail_weight = jnp.exp(end_decay[:, None] - cum_decay)
        local_state = jnp.einsum('shd,she->hde', key_bfloat * tail_weight.T[:, :, None], value_bfloat, precision=hi_prec)
        new_state = jnp.exp(end_decay)[:, None, None] * state + local_state
        return (new_state, inner_out + carried)
    initial_state = jnp.zeros((PAIRED_KV_PARTS, HEAD_SIZE, HEAD_SIZE), jnp.float32)
    unused_state, linear_out = lax.scan(linear_block, initial_state, (query_single, key_single, value_single, blocked_decay))
    linear_heads = linear_out.reshape(SEGMENT_ITEMS, QUERY_HEADS, HEAD_SIZE)
    mean_square = lax.optimization_barrier(jnp.mean(linear_heads * linear_heads, axis=2, keepdims=True))
    normed = (linear_heads / jnp.sqrt(mean_square + 1e-06)).reshape(SEGMENT_ITEMS, MODEL_SPAN) * lin_gain
    keys_padded = jnp.concatenate([jnp.zeros((WINDOW_KEYS, PAIRED_KV_PARTS * HEAD_SIZE), jnp.bfloat16), key_tensor], axis=0)
    values_padded = jnp.concatenate([jnp.zeros((WINDOW_KEYS, PAIRED_KV_PARTS * HEAD_SIZE), jnp.bfloat16), value_tensor], axis=0)

    def window_block(begin_offset):
        query_bfloat = lax.dynamic_slice_in_dim(queries, begin_offset, block_length, 0).astype(jnp.float32).reshape(block_length, PAIRED_KV_PARTS, group_extent, HEAD_SIZE)
        key_bfloat = lax.dynamic_slice_in_dim(keys_padded, begin_offset, block_length + WINDOW_KEYS, 0).astype(jnp.float32).reshape(block_length + WINDOW_KEYS, PAIRED_KV_PARTS, HEAD_SIZE)
        value_bfloat = lax.dynamic_slice_in_dim(values_padded, begin_offset, block_length + WINDOW_KEYS, 0).astype(jnp.float32).reshape(block_length + WINDOW_KEYS, PAIRED_KV_PARTS, HEAD_SIZE)
        raw_scores = jnp.einsum('thgd,shd->hgts', query_bfloat, key_bfloat) * scale_multiplier
        key_pos = begin_offset - WINDOW_KEYS + jnp.arange(block_length + WINDOW_KEYS, dtype=jnp.int32)
        query_pos = begin_offset + jnp.arange(block_length, dtype=jnp.int32)
        distance = query_pos[:, None] - key_pos[None, :]
        allowed = (distance >= 0) & (distance < WINDOW_KEYS) & (key_pos[None, :] >= 0)
        masked = jnp.where(allowed[None, None], raw_scores, -jnp.inf)
        row_max = lax.optimization_barrier(jnp.max(masked, axis=3, keepdims=True))
        expo_scores = jnp.exp(masked - row_max)
        probs = (expo_scores / lax.optimization_barrier(jnp.sum(expo_scores, axis=3, keepdims=True))).astype(jnp.bfloat16)
        window_out = jnp.einsum('hgts,shd->thgd', probs.astype(jnp.float32), value_bfloat)
        return window_out.reshape(block_length, MODEL_SPAN)
    starts = (jnp.arange(block_number) * block_length).astype(jnp.int32)
    window = lax.map(window_block, starts).reshape(SEGMENT_ITEMS, MODEL_SPAN)
    attn = (normed + window).astype(jnp.bfloat16)
    capacity = MOST * N_WIDE * N_NARROW
    block_units = FF // QUART
    flat_routes = routes.reshape(-1)
    gate_padded = jnp.concatenate([route_weight.reshape(-1), jnp.zeros((1,), jnp.float32)])
    attn_padded = jnp.concatenate([attn, jnp.zeros((1, MODEL_SPAN), jnp.bfloat16)], axis=0)

    def expert_step(total, expert):
        index_list = jnp.nonzero(flat_routes == expert, size=capacity, fill_value=SEGMENT_ITEMS * TOP)[0].astype(jnp.int32)
        token_ids = (index_list // TOP).astype(jnp.int32)
        token_rows = attn_padded[token_ids]
        gates = gate_padded[index_list]
        up_cols = lax.dynamic_slice_in_dim(w_up, (expert * FF).astype(jnp.int32), FF, 1)
        down_rows = lax.dynamic_slice_in_dim(w_down, (expert * FF).astype(jnp.int32), FF, 0)
        hidden = jax.nn.silu(jnp.dot(token_rows, up_cols, preferred_element_type=jnp.float32)).astype(jnp.bfloat16)
        summed = jnp.zeros((capacity, MODEL_SPAN), jnp.float32)
        for block_no in range(QUART):
            piece = jnp.dot(hidden[:, block_no * block_units:(block_no + 1) * block_units], down_rows[block_no * block_units:(block_no + 1) * block_units], preferred_element_type=jnp.float32)
            piece = lax.optimization_barrier(piece.astype(jnp.bfloat16))
            summed = summed + piece.astype(jnp.float32)
        return (total.at[token_ids].add(gates[:, None] * summed), None)
    moe_total, unused_out = lax.scan(expert_step, jnp.zeros((SEGMENT_ITEMS + 1, MODEL_SPAN), jnp.float32), jnp.arange(EXPERTS, dtype=jnp.int32))
    moe = moe_total[:SEGMENT_ITEMS]
    return (attn.astype(jnp.float32) + moe).astype(jnp.bfloat16)
```

```python
import functools

import jax
import jax.numpy as jnp
import numpy as np
from jax import lax
from jax.experimental import pallas as pl
from jax.experimental.pallas import tpu as pltpu
from jax.sharding import PartitionSpec as P

FF = 1408
EXPERTS = 32
TOP = 2
QUART = 4
WINDOW_KEYS = 128
MOST = 12
MESH = pl.DeviceIdType.MESH


def dot32(a, b):
    return jnp.dot(a, b, preferred_element_type=jnp.float32)


def slot_tables(wide_count, local_experts, blocks_each, rows):
    expert = np.full((wide_count, rows), -1, np.int32)
    rank = np.full((wide_count, rows), -1, np.int32)
    for d in range(wide_count):
        for e in range(local_experts):
            block = (d * local_experts + e) * blocks_each
            expert[d, e * MOST : (e + 1) * MOST] = block // QUART
            rank[d, e * MOST : (e + 1) * MOST] = np.arange(MOST)
    return expert.reshape(-1), rank.reshape(-1)


def expert_order(wide_count, local_experts, rows):
    order = np.zeros((local_experts, wide_count * MOST, wide_count * rows), np.float32)
    for e in range(local_experts):
        for d in range(wide_count):
            for m in range(MOST):
                order[e, d * MOST + m, d * rows + e * MOST + m] = 1
    return order


def moe_kernel(wide_count, local_experts, chunk, *refs):
    (
        attn_ref, routes_ref, routes_t_ref, gate_ref, slot_row_ref, slot_col_ref, order_ref, back_ref,
        up_hbm, down_hbm, out_ref,
        up, down, pick, send, recv, result, back, returned, gates_hi, gates_lo,
        up_sem, down_sem, send_sem, recv_sem, send_sem2, recv_sem2,
    ) = refs
    me = lax.axis_index("wide")
    hidden_width = up.shape[2]
    tok_count, width = attn_ref.shape
    rows = send.shape[1]
    slots = wide_count * rows

    def up_copy(e):
        cols = slice(e * hidden_width, (e + 1) * hidden_width)
        src = up_hbm if local_experts == 1 else up_hbm.at[:, cols]
        return pltpu.make_async_copy(src, up.at[e], up_sem.at[e])

    def down_copy(e):
        src = down_hbm.at[e * hidden_width : (e + 1) * hidden_width, :]
        return pltpu.make_async_copy(src, down.at[e], down_sem.at[e])

    barrier = pltpu.get_barrier_semaphore()

    @pl.loop(1, wide_count)
    def _(k):
        peer = lax.rem(me + k, wide_count)
        pl.semaphore_signal(barrier, inc=1, device_id={"wide": peer}, device_id_type=MESH)

    before = (
        lax.broadcasted_iota(jnp.int32, (tok_count, tok_count), 0)
        < lax.broadcasted_iota(jnp.int32, (tok_count, tok_count), 1)
    ).astype(jnp.bfloat16)
    after = (
        lax.broadcasted_iota(jnp.int32, (tok_count, tok_count), 0)
        > lax.broadcasted_iota(jnp.int32, (tok_count, tok_count), 1)
    ).astype(jnp.bfloat16)
    expert_col = slot_col_ref[:, 0:1]
    rank_col = slot_col_ref[:, 1:2]
    named_t = (routes_t_ref[0:1, :] == expert_col) | (routes_t_ref[1:2, :] == expert_col)
    rank_t = dot32(named_t.astype(jnp.bfloat16), before)
    picked_t = named_t & (rank_t == rank_col.astype(jnp.float32))
    pick[...] = picked_t.astype(jnp.bfloat16).reshape(pick.shape)

    pl.semaphore_wait(barrier, wide_count - 1)

    def outgoing(peer):
        return pltpu.make_async_remote_copy(
            src_ref=send.at[peer], dst_ref=recv.at[me], send_sem=send_sem.at[peer],
            recv_sem=recv_sem.at[me], device_id={"wide": peer}, device_id_type=MESH,
        )

    def incoming(peer):
        return pltpu.make_async_remote_copy(
            src_ref=send.at[peer], dst_ref=recv.at[peer], send_sem=send_sem.at[peer],
            recv_sem=recv_sem.at[peer], device_id={"wide": peer}, device_id_type=MESH,
        )

    @pl.loop(1, wide_count)
    def _(k):
        peer = lax.rem(me + k, wide_count)
        send[peer] = dot32(pick[peer], attn_ref[...]).astype(jnp.bfloat16)
        outgoing(peer).start()

    for e in range(local_experts):
        up_copy(e).start()
    for e in range(local_experts):
        down_copy(e).start()
    recv[me] = dot32(pick[me], attn_ref[...]).astype(jnp.bfloat16)

    expert_row = slot_row_ref[0:1, :]
    rank_row = slot_row_ref[1:2, :]
    first = routes_ref[:, 0:1] == expert_row
    second = routes_ref[:, 1:2] == expert_row
    rank = dot32(after, (first | second).astype(jnp.bfloat16))
    gate = jnp.where(first, gate_ref[:, 0:1], 0.0) + jnp.where(second, gate_ref[:, 1:2], 0.0)
    gate = jnp.where(rank == rank_row.astype(jnp.float32), gate, 0.0)
    high = gate.astype(jnp.bfloat16)
    gates_hi[...] = high
    gates_lo[...] = (gate - high.astype(jnp.float32)).astype(jnp.bfloat16)

    @pl.loop(1, wide_count)
    def _(k):
        peer = lax.rem(me + k, wide_count)
        incoming(peer).wait_recv()

    for e in range(local_experts):
        up_copy(e).wait()
    for e in range(local_experts):
        down_copy(e).wait()
    chunks = result.shape[1] // chunk

    @pl.loop(0, local_experts * chunks)
    def _(step):
        e = step // chunks
        at = pl.ds(pl.multiple_of((step % chunks) * chunk, chunk), chunk)
        everything = recv.reshape(slots, width)
        if local_experts > 1:
            token_rows = dot32(order_ref[e, at, :], everything[...]).astype(jnp.bfloat16)
        else:
            token_rows = everything[at, :]
        hidden = dot32(token_rows, up[e])
        hidden = (hidden * (1.0 / (1.0 + jnp.exp(-hidden)))).astype(jnp.bfloat16)
        result[e, at, :] = dot32(hidden, down[e]).astype(jnp.bfloat16)

    def homeward(peer, mine):
        return pltpu.make_async_remote_copy(
            src_ref=back.at[peer], dst_ref=returned.at[mine], send_sem=send_sem2.at[peer],
            recv_sem=recv_sem2.at[mine], device_id={"wide": peer}, device_id_type=MESH,
        )

    def rows_for(peer):
        flat = result.reshape(result.shape[0] * result.shape[1], width)
        if local_experts > 1:
            return dot32(back_ref[peer], flat[...]).astype(jnp.bfloat16)
        return flat[pl.ds(pl.multiple_of(peer * rows, rows), rows), :]

    @pl.loop(1, wide_count)
    def _(k):
        peer = lax.rem(me + k, wide_count)
        back[peer] = rows_for(peer)
        homeward(peer, me).start()

    returned[me] = rows_for(me)

    @pl.loop(1, wide_count)
    def _(k):
        peer = lax.rem(me + k, wide_count)
        homeward(peer, peer).wait_recv()

    columns = 512

    @pl.loop(0, width // columns)
    def _(c):
        at = pl.ds(pl.multiple_of(c * columns, columns), columns)
        block = returned.reshape(slots, width)[:, at]
        moe = dot32(gates_hi[...], block) + dot32(gates_lo[...], block)
        out_ref[:, at] = (attn_ref[:, at].astype(jnp.float32) + moe).astype(jnp.bfloat16)

    @pl.loop(1, wide_count)
    def _(k):
        peer = lax.rem(me + k, wide_count)
        outgoing(peer).wait_send()
        homeward(peer, me).wait_send()


def moe_layer(attn, routes, route_weight, w_up, w_down):
    wide_count = lax.axis_size("wide")
    tok_count, width = attn.shape
    units = w_up.shape[1]
    hidden_width = min(units, FF)
    local_experts = units // hidden_width
    blocks_each = hidden_width * QUART // FF
    rows = -(-local_experts * MOST // 16) * 16
    slots = wide_count * rows
    expert, rank = slot_tables(wide_count, local_experts, blocks_each, rows)
    slot_row = np.stack([expert, rank])
    if local_experts > 1:
        order = expert_order(wide_count, local_experts, rows)
        result_rows = wide_count * MOST
        flat = order.reshape(local_experts * result_rows, slots)
        order_back = flat.T.reshape(wide_count, rows, local_experts * result_rows)
    else:
        order = np.zeros((1, 16, 128), np.float32)
        order_back = order
        result_rows = slots
    chunk = result_rows if result_rows <= 128 else 128
    bf = jnp.bfloat16
    vmem = pl.BlockSpec(memory_space=pltpu.VMEM)
    hbm = pl.BlockSpec(memory_space=pltpu.HBM)
    dma = pltpu.SemaphoreType.DMA
    return pl.pallas_call(
        functools.partial(moe_kernel, wide_count, local_experts, chunk),
        out_shape=jax.ShapeDtypeStruct((tok_count, width), bf),
        in_specs=[vmem] * 8 + [hbm] * 2,
        out_specs=vmem,
        scratch_shapes=[
            pltpu.VMEM((local_experts, width, hidden_width), bf),
            pltpu.VMEM((local_experts, hidden_width, width), bf),
            pltpu.VMEM((wide_count, rows, tok_count), bf),
            pltpu.VMEM((wide_count, rows, width), bf),
            pltpu.VMEM((wide_count, rows, width), bf),
            pltpu.VMEM((local_experts, result_rows, width), bf),
            pltpu.VMEM((wide_count, rows, width), bf),
            pltpu.VMEM((wide_count, rows, width), bf),
            pltpu.VMEM((tok_count, slots), bf),
            pltpu.VMEM((tok_count, slots), bf),
            dma((local_experts,)),
            dma((local_experts,)),
            dma((wide_count,)),
            dma((wide_count,)),
            dma((wide_count,)),
            dma((wide_count,)),
        ],
        compiler_params=pltpu.CompilerParams(
            collective_id=0, has_side_effects=True, vmem_limit_bytes=60 * 1024 * 1024
        ),
        name="moe",
    )(
        attn, routes, routes.T, route_weight, jnp.asarray(slot_row), jnp.asarray(slot_row.T),
        jnp.asarray(order, bf), jnp.asarray(order_back, bf), w_up, w_down,
    )


def passed_along(x, axis, by):
    peers = lax.axis_size(axis)
    pairs = [(i, i + by) for i in range(peers) if 0 <= i + by < peers]
    return lax.ppermute(x, axis, pairs)


def carried_in(end_decay, local_state):
    axis = ("wide", "narrow")
    peers, here = lax.axis_size(axis), lax.axis_index(axis)
    decays = lax.all_gather(end_decay, axis)
    states = lax.all_gather(local_state, axis)
    k = jnp.arange(peers)
    between = (k[None, :] > k[:, None]) & (k[None, :] < here)
    gap = jnp.sum(jnp.where(between[:, :, None], decays[None], 0.0), axis=1)
    weight = jnp.where((k < here)[:, None], jnp.exp(gap), 0.0)
    return jnp.sum(weight[:, :, None, None] * states, axis=0)


def per_device(
    queries, key_tensor, value_tensor, decay_logarithm, lin_gain, routes, route_weight, w_up, w_down
):
    tok_count = queries.shape[0]
    model_width = queries.shape[1]
    kv_heads = decay_logarithm.shape[0]
    head_dim = key_tensor.shape[1] // kv_heads
    group_extent = model_width // (kv_heads * head_dim)
    scale_multiplier = head_dim ** (-0.5)
    hi_prec = lax.Precision.HIGHEST
    query_single = queries.astype(jnp.float32).reshape(tok_count, kv_heads, group_extent, head_dim)
    key_single = (
        key_tensor.astype(jnp.float32).reshape(tok_count, kv_heads, head_dim) * scale_multiplier
    )
    value_single = value_tensor.astype(jnp.float32).reshape(tok_count, kv_heads, head_dim)
    position = jnp.arange(tok_count)
    causal = position[:, None] >= position[None, :]
    cum_decay = jnp.sum(jnp.where(causal[None], decay_logarithm[:, None, :], 0.0), axis=2)
    end_decay = cum_decay[:, -1]
    gap_decay = cum_decay[:, :, None] - cum_decay[:, None, :]
    weight_mask = jnp.where(causal[None], jnp.exp(jnp.where(causal[None], gap_decay, 0.0)), 0.0)
    inner_scores = (
        jnp.einsum("thgd,shd->hgts", query_single, key_single, precision=hi_prec)
        * weight_mask[:, None]
    )
    inner_out = jnp.einsum("hgts,shd->thgd", inner_scores, value_single, precision=hi_prec)
    tail_weight = jnp.exp(end_decay[:, None] - cum_decay)
    local_state = jnp.einsum(
        "shd,she->hde", key_single * tail_weight.T[:, :, None], value_single, precision=hi_prec
    )
    incoming = carried_in(end_decay, local_state)
    carried = (
        jnp.einsum("thgd,hde->thge", query_single, incoming, precision=hi_prec)
        * jnp.exp(cum_decay).T[:, :, None, None]
    )
    linear_heads = (inner_out + carried).reshape(tok_count, -1, head_dim)
    mean_square = jnp.mean(linear_heads * linear_heads, axis=2, keepdims=True)
    normed = (linear_heads / jnp.sqrt(mean_square + 1e-06)).reshape(
        tok_count, model_width
    ) * lin_gain
    prev_keys, prev_values = passed_along((key_tensor, value_tensor), ("wide", "narrow"), 1)
    all_keys = jnp.concatenate([prev_keys, key_tensor], axis=0).reshape(-1, kv_heads, head_dim)
    all_values = jnp.concatenate([prev_values, value_tensor], axis=0).reshape(
        -1, kv_heads, head_dim
    )
    query_bfloat = queries.reshape(tok_count, kv_heads, group_extent, head_dim)
    raw_scores = (
        jnp.einsum("thgd,shd->hgts", query_bfloat, all_keys, preferred_element_type=jnp.float32)
        * scale_multiplier
    )
    key_pos = jnp.arange(WINDOW_KEYS + tok_count) - WINDOW_KEYS
    distance = position[:, None] - key_pos[None, :]
    device_index = lax.axis_index(("wide", "narrow"))
    allowed = (
        (distance >= 0) & (distance < WINDOW_KEYS) & ((key_pos[None, :] >= 0) | (device_index > 0))
    )
    masked = jnp.where(allowed[None, None], raw_scores, -jnp.inf)
    row_max = jnp.max(masked, axis=3, keepdims=True)
    expo_scores = jnp.exp(masked - row_max)
    probs = (expo_scores / jnp.sum(expo_scores, axis=3, keepdims=True)).astype(jnp.bfloat16)
    window_out = jnp.einsum(
        "hgts,shd->thgd", probs, all_values, preferred_element_type=jnp.float32
    ).reshape(tok_count, model_width)
    attn = (normed + window_out).astype(jnp.bfloat16)
    return moe_layer(attn, routes, route_weight, w_up, w_down)


def solution(mesh):
    in_specs = (
        P(("wide", "narrow"), None),
        P(("wide", "narrow"), None),
        P(("wide", "narrow"), None),
        P(None, ("wide", "narrow")),
        P(),
        P(("wide", "narrow"), None),
        P(("wide", "narrow"), None),
        P(None, "wide"),
        P("wide", None),
    )
    out_specs = P(("wide", "narrow"), None)
    return jax.shard_map(
        per_device, mesh=mesh, in_specs=in_specs, out_specs=out_specs, check_vma=False
    )
```

```python
import functools

import jax
import jax.numpy as jnp
import numpy as np
from jax import lax
from jax.experimental import pallas as pl
from jax.experimental.pallas import tpu as pltpu
from jax.sharding import PartitionSpec as P

FF = 1408
EXPERTS = 32
TOP = 2
QUART = 4
WINDOW_KEYS = 128
MOST = 12
MESH = pl.DeviceIdType.MESH


def dot32(a, b):
    return jnp.dot(a, b, preferred_element_type=jnp.float32)


def slot_tables(wide_count, local_experts, blocks_each, rows):
    expert = np.full((wide_count, rows), -1, np.int32)
    rank = np.full((wide_count, rows), -1, np.int32)
    for d in range(wide_count):
        for e in range(local_experts):
            block = (d * local_experts + e) * blocks_each
            expert[d, e * MOST : (e + 1) * MOST] = block // QUART
            rank[d, e * MOST : (e + 1) * MOST] = np.arange(MOST)
    return expert.reshape(-1), rank.reshape(-1)


def expert_order(wide_count, local_experts, rows):
    order = np.zeros((local_experts, wide_count * MOST, wide_count * rows), np.float32)
    for e in range(local_experts):
        for d in range(wide_count):
            for m in range(MOST):
                order[e, d * MOST + m, d * rows + e * MOST + m] = 1
    return order


def split(x):
    high = x.astype(jnp.bfloat16)
    return high, (x - high.astype(jnp.float32)).astype(jnp.bfloat16)


def dot_split(a, b):
    high, low = split(a)
    return dot32(high, b) + dot32(low, b)


def dot_t(a, b):
    return lax.dot_general(a, b, (((1,), (1,)), ((), ())), preferred_element_type=jnp.float32)


def layer_kernel(wide_count, narrow_count, local_experts, chunk, *refs):
    (
        query_ref, key_ref, value_ref, decay_ref, decay_t_ref, gain_ref,
        routes_ref, routes_t_ref, gate_ref, slot_row_ref, slot_col_ref, order_ref, back_ref,
        up_hbm, down_hbm, out_ref,
        prev_key, prev_value, out1, in1, out2, in2, out3, in3, state_hi, state_lo, linear, window,
        attn_ref,
        up, down, pick, send, recv, result, back, returned, gates_hi, gates_lo,
        kv_send, kv_recv, s1, r1, s2, r2, s3, r3,
        up_sem, down_sem, send_sem, recv_sem, send_sem2, recv_sem2,
    ) = refs
    me = lax.axis_index("wide")
    here = lax.axis_index("narrow")
    hidden_width = up.shape[2]
    tok_count, width = query_ref.shape
    kv_heads = decay_ref.shape[0]
    head_dim = key_ref.shape[1] // kv_heads
    group = width // (kv_heads * head_dim)
    part_rows = head_dim // narrow_count
    scale = head_dim ** (-0.5)
    rows = send.shape[1]
    slots = wide_count * rows
    is_first = (me == 0) & (here == 0)
    is_last = (me == wide_count - 1) & (here == narrow_count - 1)
    from_before = (here == 0) & (me > 0)
    to_next = (here == narrow_count - 1) & (me < wide_count - 1)

    def up_copy(e):
        cols = slice(e * hidden_width, (e + 1) * hidden_width)
        src = up_hbm if local_experts == 1 else up_hbm.at[:, cols]
        return pltpu.make_async_copy(src, up.at[e], up_sem.at[e])

    def down_copy(e):
        src = down_hbm.at[e * hidden_width : (e + 1) * hidden_width, :]
        return pltpu.make_async_copy(src, down.at[e], down_sem.at[e])

    barrier = pltpu.get_barrier_semaphore()

    @pl.loop(1, wide_count)
    def _(k):
        peer = lax.rem(me + k, wide_count)
        pl.semaphore_signal(barrier, inc=1, device_id={"wide": peer}, device_id_type=MESH)

    for k in range(1, narrow_count):
        peer = lax.rem(here + k, narrow_count)
        pl.semaphore_signal(barrier, inc=1, device_id={"narrow": peer}, device_id_type=MESH)

    @pl.when(from_before)
    def _():
        target = {"wide": me - 1, "narrow": narrow_count - 1}
        pl.semaphore_signal(barrier, inc=1, device_id=target, device_id_type=MESH)

    @pl.when(to_next)
    def _():
        target = {"wide": me + 1, "narrow": 0}
        pl.semaphore_signal(barrier, inc=1, device_id=target, device_id_type=MESH)

    for e in range(local_experts):
        up_copy(e).start()
    for e in range(local_experts):
        down_copy(e).start()

    at_row = lax.broadcasted_iota(jnp.int32, (tok_count, tok_count), 0)
    at_col = lax.broadcasted_iota(jnp.int32, (tok_count, tok_count), 1)
    causal = at_col <= at_row
    sums = []
    for h in range(kv_heads):
        decay_row = decay_ref[h : h + 1, :]
        decay_col = decay_t_ref[:, h : h + 1]
        cum_col = jnp.sum(jnp.where(causal, decay_row, 0.0), axis=1, keepdims=True)
        cum_row = jnp.sum(jnp.where(at_row <= at_col, decay_col, 0.0), axis=0, keepdims=True)
        rest = jnp.sum(jnp.where(at_col > at_row, decay_row, 0.0), axis=1, keepdims=True)
        total = jnp.sum(decay_row, axis=1, keepdims=True)
        sums.append((cum_col, cum_row))
        lanes = slice(h * head_dim, (h + 1) * head_dim)
        faded = key_ref[:, lanes].astype(jnp.float32) * (scale * jnp.exp(rest))
        state = dot_split(faded.T, value_ref[:, lanes])
        for j in range(narrow_count):
            out1[j, h, 0:part_rows, :] = state[j * part_rows : (j + 1) * part_rows, :]
            out1[j, h, part_rows:, :] = jnp.broadcast_to(total, (8, head_dim))

    extra = from_before.astype(jnp.int32) + to_next.astype(jnp.int32)
    pl.semaphore_wait(barrier, wide_count - 1 + narrow_count - 1 + extra)

    next_here = lax.rem(here + 1, narrow_count)
    next_wide = lax.rem(me + to_next.astype(jnp.int32), wide_count)

    def pass_on(which):
        src, dst = ((key_ref, prev_key), (value_ref, prev_value))[which]
        return pltpu.make_async_remote_copy(
            src_ref=src, dst_ref=dst, send_sem=kv_send.at[which], recv_sem=kv_recv.at[which],
            device_id={"wide": next_wide, "narrow": next_here}, device_id_type=MESH,
        )

    def swap1(peer, slot):
        return pltpu.make_async_remote_copy(
            src_ref=out1.at[peer], dst_ref=in1.at[slot], send_sem=s1.at[peer],
            recv_sem=r1.at[slot], device_id={"narrow": peer}, device_id_type=MESH,
        )

    def swap2(peer, slot):
        return pltpu.make_async_remote_copy(
            src_ref=out2, dst_ref=in2.at[slot], send_sem=s2.at[peer],
            recv_sem=r2.at[slot], device_id={"wide": peer}, device_id_type=MESH,
        )

    def swap3(peer, slot):
        return pltpu.make_async_remote_copy(
            src_ref=out3.at[peer], dst_ref=in3.at[slot], send_sem=s3.at[peer],
            recv_sem=r3.at[slot], device_id={"narrow": peer}, device_id_type=MESH,
        )

    near = [lax.rem(here + k, narrow_count) for k in range(1, narrow_count)]
    for peer in near:
        swap1(peer, here).start()

    @pl.when(jnp.logical_not(is_last))
    def _():
        pass_on(0).start()
        pass_on(1).start()

    in1[here] = out1[here]

    before = (
        lax.broadcasted_iota(jnp.int32, (tok_count, tok_count), 0)
        < lax.broadcasted_iota(jnp.int32, (tok_count, tok_count), 1)
    ).astype(jnp.bfloat16)
    after = (
        lax.broadcasted_iota(jnp.int32, (tok_count, tok_count), 0)
        > lax.broadcasted_iota(jnp.int32, (tok_count, tok_count), 1)
    ).astype(jnp.bfloat16)
    expert_col = slot_col_ref[:, 0:1]
    rank_col = slot_col_ref[:, 1:2]
    named_t = (routes_t_ref[0:1, :] == expert_col) | (routes_t_ref[1:2, :] == expert_col)
    rank_t = dot32(named_t.astype(jnp.bfloat16), before)
    picked_t = named_t & (rank_t == rank_col.astype(jnp.float32))
    pick[...] = picked_t.astype(jnp.bfloat16).reshape(pick.shape)

    expert_row = slot_row_ref[0:1, :]
    rank_row = slot_row_ref[1:2, :]
    first = routes_ref[:, 0:1] == expert_row
    second = routes_ref[:, 1:2] == expert_row
    rank = dot32(after, (first | second).astype(jnp.bfloat16))
    gate = jnp.where(first, gate_ref[:, 0:1], 0.0) + jnp.where(second, gate_ref[:, 1:2], 0.0)
    gate = jnp.where(rank == rank_row.astype(jnp.float32), gate, 0.0)
    high = gate.astype(jnp.bfloat16)
    gates_hi[...] = high
    gates_lo[...] = (gate - high.astype(jnp.float32)).astype(jnp.bfloat16)

    for peer in near:
        swap1(peer, peer).wait_recv()
    for h in range(kv_heads):
        total = jnp.zeros((part_rows, head_dim), jnp.float32)
        log_decay = jnp.zeros((8, head_dim), jnp.float32)
        for j in range(narrow_count):
            fade = in1[j, h, part_rows:, :]
            total = jnp.exp(fade[0:1, :]) * total + in1[j, h, 0:part_rows, :]
            log_decay = log_decay + fade
        out2[h, 0:part_rows, :] = total
        out2[h, part_rows:, :] = log_decay

    @pl.loop(1, wide_count)
    def _(k):
        peer = lax.rem(me + k, wide_count)
        swap2(peer, me).start()

    in2[me] = out2[...]

    @pl.when(is_first)
    def _():
        prev_key[...] = jnp.zeros_like(prev_key)
        prev_value[...] = jnp.zeros_like(prev_value)

    @pl.when(jnp.logical_not(is_first))
    def _():
        pass_on(0).wait_recv()
        pass_on(1).wait_recv()

    no_earlier = jnp.where(is_first, 1, 0)
    reach = causal | (jnp.full((tok_count, tok_count), 1, jnp.int32) * no_earlier == 0)
    for h in range(kv_heads):
        lanes = slice(h * head_dim, (h + 1) * head_dim)
        cum_col, cum_row = sums[h]
        fading = jnp.where(causal, jnp.exp(jnp.where(causal, cum_col - cum_row, 0.0)), 0.0)

        @pl.loop(0, group)
        def _(g):
            at = pl.ds(pl.multiple_of((h * group + g) * head_dim, head_dim), head_dim)
            q = query_ref[:, at]
            own = dot_t(q, key_ref[:, lanes]) * scale
            older = dot_t(q, prev_key[:, lanes]) * scale
            linear[:, at] = dot_split(own * fading, value_ref[:, lanes])
            score = jnp.where(reach, jnp.where(causal, own, older), -jnp.inf)
            expo = jnp.exp(score - jnp.max(score, axis=1, keepdims=True))
            probs = expo / jnp.sum(expo, axis=1, keepdims=True)
            window[:, at] = dot32(
                jnp.where(causal, probs, 0.0).astype(jnp.bfloat16), value_ref[:, lanes]
            ) + dot32(jnp.where(causal, 0.0, probs).astype(jnp.bfloat16), prev_value[:, lanes])

    @pl.loop(1, wide_count)
    def _(k):
        peer = lax.rem(me + k, wide_count)
        swap2(peer, peer).wait_recv()

    for h in range(kv_heads):
        def carry(w, held):
            fresh = jnp.exp(in2[w, h, part_rows : part_rows + 1, :]) * held
            return fresh + in2[w, h, 0:part_rows, :]

        held = lax.fori_loop(0, me, carry, jnp.zeros((part_rows, head_dim), jnp.float32))
        for j in range(narrow_count):
            out3[j, h] = held
            held = jnp.exp(in1[j, h, part_rows : part_rows + 1, :]) * held
            held = held + in1[j, h, 0:part_rows, :]
    for peer in near:
        swap3(peer, here).start()
    in3[here] = out3[here]
    for peer in near:
        swap3(peer, peer).wait_recv()

    for h in range(kv_heads):
        for j in range(narrow_count):
            high, low = split(in3[j, h])
            state_hi[h, j * part_rows : (j + 1) * part_rows, :] = high
            state_lo[h, j * part_rows : (j + 1) * part_rows, :] = low
        grown = jnp.exp(sums[h][0])

        @pl.loop(0, group)
        def _(g):
            at = pl.ds(pl.multiple_of((h * group + g) * head_dim, head_dim), head_dim)
            q = query_ref[:, at]
            heads = linear[:, at] + (dot32(q, state_hi[h]) + dot32(q, state_lo[h])) * grown
            square = jnp.mean(heads * heads, axis=1, keepdims=True)
            normed = heads / jnp.sqrt(square + 1e-06) * gain_ref[0:1, at]
            attn_ref[:, at] = (normed + window[:, at]).astype(jnp.bfloat16)

    def outgoing(peer):
        return pltpu.make_async_remote_copy(
            src_ref=send.at[peer], dst_ref=recv.at[me], send_sem=send_sem.at[peer],
            recv_sem=recv_sem.at[me], device_id={"wide": peer}, device_id_type=MESH,
        )

    def incoming(peer):
        return pltpu.make_async_remote_copy(
            src_ref=send.at[peer], dst_ref=recv.at[peer], send_sem=send_sem.at[peer],
            recv_sem=recv_sem.at[peer], device_id={"wide": peer}, device_id_type=MESH,
        )

    @pl.loop(1, wide_count)
    def _(k):
        peer = lax.rem(me + k, wide_count)
        send[peer] = dot32(pick[peer], attn_ref[...]).astype(jnp.bfloat16)
        outgoing(peer).start()

    recv[me] = dot32(pick[me], attn_ref[...]).astype(jnp.bfloat16)

    @pl.loop(1, wide_count)
    def _(k):
        peer = lax.rem(me + k, wide_count)
        incoming(peer).wait_recv()

    for e in range(local_experts):
        up_copy(e).wait()
    for e in range(local_experts):
        down_copy(e).wait()
    chunks = result.shape[1] // chunk

    @pl.loop(0, local_experts * chunks)
    def _(step):
        e = step // chunks
        at = pl.ds(pl.multiple_of((step % chunks) * chunk, chunk), chunk)
        everything = recv.reshape(slots, width)
        if local_experts > 1:
            token_rows = dot32(order_ref[e, at, :], everything[...]).astype(jnp.bfloat16)
        else:
            token_rows = everything[at, :]
        hidden = dot32(token_rows, up[e])
        hidden = (hidden * (1.0 / (1.0 + jnp.exp(-hidden)))).astype(jnp.bfloat16)
        result[e, at, :] = dot32(hidden, down[e]).astype(jnp.bfloat16)

    def homeward(peer, mine):
        return pltpu.make_async_remote_copy(
            src_ref=back.at[peer], dst_ref=returned.at[mine], send_sem=send_sem2.at[peer],
            recv_sem=recv_sem2.at[mine], device_id={"wide": peer}, device_id_type=MESH,
        )

    def rows_for(peer):
        flat = result.reshape(result.shape[0] * result.shape[1], width)
        if local_experts > 1:
            return dot32(back_ref[peer], flat[...]).astype(jnp.bfloat16)
        return flat[pl.ds(pl.multiple_of(peer * rows, rows), rows), :]

    @pl.loop(1, wide_count)
    def _(k):
        peer = lax.rem(me + k, wide_count)
        back[peer] = rows_for(peer)
        homeward(peer, me).start()

    returned[me] = rows_for(me)

    @pl.loop(1, wide_count)
    def _(k):
        peer = lax.rem(me + k, wide_count)
        homeward(peer, peer).wait_recv()

    columns = 512

    @pl.loop(0, width // columns)
    def _(c):
        at = pl.ds(pl.multiple_of(c * columns, columns), columns)
        block = returned.reshape(slots, width)[:, at]
        moe = dot32(gates_hi[...], block) + dot32(gates_lo[...], block)
        out_ref[:, at] = (attn_ref[:, at].astype(jnp.float32) + moe).astype(jnp.bfloat16)

    for peer in near:
        swap1(peer, here).wait_send()
        swap3(peer, here).wait_send()

    @pl.when(jnp.logical_not(is_last))
    def _():
        pass_on(0).wait_send()
        pass_on(1).wait_send()

    @pl.loop(1, wide_count)
    def _(k):
        peer = lax.rem(me + k, wide_count)
        swap2(peer, me).wait_send()
        outgoing(peer).wait_send()
        homeward(peer, me).wait_send()


def per_device(
    queries, key_tensor, value_tensor, decay_logarithm, lin_gain, routes, route_weight, w_up, w_down
):
    wide_count = lax.axis_size("wide")
    narrow_count = lax.axis_size("narrow")
    tok_count, width = queries.shape
    kv_heads = decay_logarithm.shape[0]
    head_dim = key_tensor.shape[1] // kv_heads
    part_rows = head_dim // narrow_count
    units = w_up.shape[1]
    hidden_width = min(units, FF)
    local_experts = units // hidden_width
    blocks_each = hidden_width * QUART // FF
    rows = -(-local_experts * MOST // 16) * 16
    slots = wide_count * rows
    expert, rank = slot_tables(wide_count, local_experts, blocks_each, rows)
    slot_row = np.stack([expert, rank])
    if local_experts > 1:
        order = expert_order(wide_count, local_experts, rows)
        result_rows = wide_count * MOST
        flat = order.reshape(local_experts * result_rows, slots)
        order_back = flat.T.reshape(wide_count, rows, local_experts * result_rows)
    else:
        order = np.zeros((1, 16, 128), np.float32)
        order_back = order
        result_rows = slots
    chunk = result_rows if result_rows <= 128 else 128
    bf = jnp.bfloat16
    vmem = pl.BlockSpec(memory_space=pltpu.VMEM)
    hbm = pl.BlockSpec(memory_space=pltpu.HBM)
    dma = pltpu.SemaphoreType.DMA
    return pl.pallas_call(
        functools.partial(layer_kernel, wide_count, narrow_count, local_experts, chunk),
        out_shape=jax.ShapeDtypeStruct((tok_count, width), bf),
        in_specs=[vmem] * 13 + [hbm] * 2,
        out_specs=vmem,
        scratch_shapes=[
            pltpu.VMEM(key_tensor.shape, bf),
            pltpu.VMEM(value_tensor.shape, bf),
            pltpu.VMEM((narrow_count, kv_heads, part_rows + 8, head_dim), jnp.float32),
            pltpu.VMEM((narrow_count, kv_heads, part_rows + 8, head_dim), jnp.float32),
            pltpu.VMEM((kv_heads, part_rows + 8, head_dim), jnp.float32),
            pltpu.VMEM((wide_count, kv_heads, part_rows + 8, head_dim), jnp.float32),
            pltpu.VMEM((narrow_count, kv_heads, part_rows, head_dim), jnp.float32),
            pltpu.VMEM((narrow_count, kv_heads, part_rows, head_dim), jnp.float32),
            pltpu.VMEM((kv_heads, head_dim, head_dim), bf),
            pltpu.VMEM((kv_heads, head_dim, head_dim), bf),
            pltpu.VMEM((tok_count, width), jnp.float32),
            pltpu.VMEM((tok_count, width), jnp.float32),
            pltpu.VMEM((tok_count, width), bf),
            pltpu.VMEM((local_experts, width, hidden_width), bf),
            pltpu.VMEM((local_experts, hidden_width, width), bf),
            pltpu.VMEM((wide_count, rows, tok_count), bf),
            pltpu.VMEM((wide_count, rows, width), bf),
            pltpu.VMEM((wide_count, rows, width), bf),
            pltpu.VMEM((local_experts, result_rows, width), bf),
            pltpu.VMEM((wide_count, rows, width), bf),
            pltpu.VMEM((wide_count, rows, width), bf),
            pltpu.VMEM((tok_count, slots), bf),
            pltpu.VMEM((tok_count, slots), bf),
            dma((2,)),
            dma((2,)),
            dma((narrow_count,)),
            dma((narrow_count,)),
            dma((wide_count,)),
            dma((wide_count,)),
            dma((narrow_count,)),
            dma((narrow_count,)),
            dma((local_experts,)),
            dma((local_experts,)),
            dma((wide_count,)),
            dma((wide_count,)),
            dma((wide_count,)),
            dma((wide_count,)),
        ],
        compiler_params=pltpu.CompilerParams(
            collective_id=0, has_side_effects=True, vmem_limit_bytes=62 * 1024 * 1024
        ),
        name="layer",
    )(
        queries, key_tensor, value_tensor, decay_logarithm, decay_logarithm.T, lin_gain.reshape(1, -1),
        routes, routes.T, route_weight, jnp.asarray(slot_row), jnp.asarray(slot_row.T),
        jnp.asarray(order, bf), jnp.asarray(order_back, bf), w_up, w_down,
    )


def solution(mesh):
    in_specs = (
        P(("wide", "narrow"), None),
        P(("wide", "narrow"), None),
        P(("wide", "narrow"), None),
        P(None, ("wide", "narrow")),
        P(),
        P(("wide", "narrow"), None),
        P(("wide", "narrow"), None),
        P(None, "wide"),
        P("wide", None),
    )
    out_specs = P(("wide", "narrow"), None)
    return jax.shard_map(
        per_device, mesh=mesh, in_specs=in_specs, out_specs=out_specs, check_vma=False
    )
```

```python
import functools

import jax
import jax.numpy as jnp
import numpy as np
from jax import lax
from jax.experimental import pallas as pl
from jax.experimental.pallas import tpu as pltpu
from jax.sharding import PartitionSpec as P

FF = 1408
EXPERTS = 32
TOP = 2
QUART = 4
WINDOW_KEYS = 128
MOST = 12
MESH = pl.DeviceIdType.MESH


def dot32(a, b):
    return jnp.dot(a, b, preferred_element_type=jnp.float32)


def slot_tables(wide_count, local_experts, blocks_each, rows):
    expert = np.full((wide_count, rows), -1, np.int32)
    rank = np.full((wide_count, rows), -1, np.int32)
    for d in range(wide_count):
        for e in range(local_experts):
            block = (d * local_experts + e) * blocks_each
            expert[d, e * MOST : (e + 1) * MOST] = block // QUART
            rank[d, e * MOST : (e + 1) * MOST] = np.arange(MOST)
    return expert.reshape(-1), rank.reshape(-1)


def expert_order(wide_count, local_experts, rows):
    order = np.zeros((local_experts, wide_count * MOST, wide_count * rows), np.float32)
    for e in range(local_experts):
        for d in range(wide_count):
            for m in range(MOST):
                order[e, d * MOST + m, d * rows + e * MOST + m] = 1
    return order


def split(x):
    high = x.astype(jnp.bfloat16)
    return high, (x - high.astype(jnp.float32)).astype(jnp.bfloat16)


def dot_split(a, b):
    high, low = split(a)
    return dot32(high, b) + dot32(low, b)


def dot_t(a, b):
    return lax.dot_general(a, b, (((1,), (1,)), ((), ())), preferred_element_type=jnp.float32)


def layer_kernel(wide_count, narrow_count, local_experts, chunk, *refs):
    (
        query_ref, key_ref, value_ref, decay_ref, decay_t_ref, gain_ref,
        routes_ref, routes_t_ref, gate_ref, slot_row_ref, slot_col_ref, order_ref, back_ref,
        up_hbm, down_hbm, out_ref,
        prev_key, prev_value, out1, in1, out2, in2, out3, in3, state_hi, state_lo, linear, window,
        attn_ref,
        up, down, pick, send, recv, hidden_sum, hidden, result, back, returned, gates_hi, gates_lo,
        kv_send, kv_recv, s1, r1, s2, r2, s3, r3,
        up_sem, down_sem, send_sem, recv_sem, send_sem2, recv_sem2,
    ) = refs
    me = lax.axis_index("wide")
    here = lax.axis_index("narrow")
    hidden_width = up.shape[2]
    tok_count, width = query_ref.shape
    kv_heads = decay_ref.shape[0]
    head_dim = key_ref.shape[1] // kv_heads
    group = width // (kv_heads * head_dim)
    part_rows = head_dim // narrow_count
    scale = head_dim ** (-0.5)
    parts_in, _, rows, columns_in = send.shape
    parts_out, _, _, columns_out = back.shape
    slots = wide_count * rows
    is_first = (me == 0) & (here == 0)
    is_last = (me == wide_count - 1) & (here == narrow_count - 1)
    from_before = (here == 0) & (me > 0)
    to_next = (here == narrow_count - 1) & (me < wide_count - 1)

    def up_copy(e):
        cols = slice(e * hidden_width, (e + 1) * hidden_width)
        src = up_hbm if local_experts == 1 else up_hbm.at[:, cols]
        return pltpu.make_async_copy(src, up.at[e], up_sem.at[e])

    def down_copy(e):
        src = down_hbm.at[e * hidden_width : (e + 1) * hidden_width, :]
        return pltpu.make_async_copy(src, down.at[e], down_sem.at[e])

    barrier = pltpu.get_barrier_semaphore()

    @pl.loop(1, wide_count)
    def _(k):
        peer = lax.rem(me + k, wide_count)
        pl.semaphore_signal(barrier, inc=1, device_id={"wide": peer}, device_id_type=MESH)

    for k in range(1, narrow_count):
        peer = lax.rem(here + k, narrow_count)
        pl.semaphore_signal(barrier, inc=1, device_id={"narrow": peer}, device_id_type=MESH)

    @pl.when(from_before)
    def _():
        target = {"wide": me - 1, "narrow": narrow_count - 1}
        pl.semaphore_signal(barrier, inc=1, device_id=target, device_id_type=MESH)

    @pl.when(to_next)
    def _():
        target = {"wide": me + 1, "narrow": 0}
        pl.semaphore_signal(barrier, inc=1, device_id=target, device_id_type=MESH)

    for e in range(local_experts):
        up_copy(e).start()
    for e in range(local_experts):
        down_copy(e).start()

    at_row = lax.broadcasted_iota(jnp.int32, (tok_count, tok_count), 0)
    at_col = lax.broadcasted_iota(jnp.int32, (tok_count, tok_count), 1)
    causal = at_col <= at_row
    sums = []
    for h in range(kv_heads):
        decay_row = decay_ref[h : h + 1, :]
        decay_col = decay_t_ref[:, h : h + 1]
        cum_col = jnp.sum(jnp.where(causal, decay_row, 0.0), axis=1, keepdims=True)
        cum_row = jnp.sum(jnp.where(at_row <= at_col, decay_col, 0.0), axis=0, keepdims=True)
        rest = jnp.sum(jnp.where(at_col > at_row, decay_row, 0.0), axis=1, keepdims=True)
        total = jnp.sum(decay_row, axis=1, keepdims=True)
        sums.append((cum_col, cum_row))
        lanes = slice(h * head_dim, (h + 1) * head_dim)
        faded = key_ref[:, lanes].astype(jnp.float32) * (scale * jnp.exp(rest))
        state = dot_split(faded.T, value_ref[:, lanes])
        for j in range(narrow_count):
            out1[j, h, 0:part_rows, :] = state[j * part_rows : (j + 1) * part_rows, :]
            out1[j, h, part_rows:, :] = jnp.broadcast_to(total, (8, head_dim))

    extra = from_before.astype(jnp.int32) + to_next.astype(jnp.int32)
    pl.semaphore_wait(barrier, wide_count - 1 + narrow_count - 1 + extra)

    next_here = lax.rem(here + 1, narrow_count)
    next_wide = lax.rem(me + to_next.astype(jnp.int32), wide_count)

    def pass_on(which):
        src, dst = ((key_ref, prev_key), (value_ref, prev_value))[which]
        return pltpu.make_async_remote_copy(
            src_ref=src, dst_ref=dst, send_sem=kv_send.at[which], recv_sem=kv_recv.at[which],
            device_id={"wide": next_wide, "narrow": next_here}, device_id_type=MESH,
        )

    def swap1(peer, slot):
        return pltpu.make_async_remote_copy(
            src_ref=out1.at[peer], dst_ref=in1.at[slot], send_sem=s1.at[peer],
            recv_sem=r1.at[slot], device_id={"narrow": peer}, device_id_type=MESH,
        )

    def swap2(peer, slot):
        return pltpu.make_async_remote_copy(
            src_ref=out2, dst_ref=in2.at[slot], send_sem=s2.at[peer],
            recv_sem=r2.at[slot], device_id={"wide": peer}, device_id_type=MESH,
        )

    def swap3(peer, slot):
        return pltpu.make_async_remote_copy(
            src_ref=out3.at[peer], dst_ref=in3.at[slot], send_sem=s3.at[peer],
            recv_sem=r3.at[slot], device_id={"narrow": peer}, device_id_type=MESH,
        )

    near = [lax.rem(here + k, narrow_count) for k in range(1, narrow_count)]
    for peer in near:
        swap1(peer, here).start()

    @pl.when(jnp.logical_not(is_last))
    def _():
        pass_on(0).start()
        pass_on(1).start()

    in1[here] = out1[here]

    before = (
        lax.broadcasted_iota(jnp.int32, (tok_count, tok_count), 0)
        < lax.broadcasted_iota(jnp.int32, (tok_count, tok_count), 1)
    ).astype(jnp.bfloat16)
    after = (
        lax.broadcasted_iota(jnp.int32, (tok_count, tok_count), 0)
        > lax.broadcasted_iota(jnp.int32, (tok_count, tok_count), 1)
    ).astype(jnp.bfloat16)
    expert_col = slot_col_ref[:, 0:1]
    rank_col = slot_col_ref[:, 1:2]
    named_t = (routes_t_ref[0:1, :] == expert_col) | (routes_t_ref[1:2, :] == expert_col)
    rank_t = dot32(named_t.astype(jnp.bfloat16), before)
    picked_t = named_t & (rank_t == rank_col.astype(jnp.float32))
    pick[...] = picked_t.astype(jnp.bfloat16).reshape(pick.shape)

    expert_row = slot_row_ref[0:1, :]
    rank_row = slot_row_ref[1:2, :]
    first = routes_ref[:, 0:1] == expert_row
    second = routes_ref[:, 1:2] == expert_row
    rank = dot32(after, (first | second).astype(jnp.bfloat16))
    gate = jnp.where(first, gate_ref[:, 0:1], 0.0) + jnp.where(second, gate_ref[:, 1:2], 0.0)
    gate = jnp.where(rank == rank_row.astype(jnp.float32), gate, 0.0)
    high = gate.astype(jnp.bfloat16)
    gates_hi[...] = high
    gates_lo[...] = (gate - high.astype(jnp.float32)).astype(jnp.bfloat16)

    for peer in near:
        swap1(peer, peer).wait_recv()
    for h in range(kv_heads):
        total = jnp.zeros((part_rows, head_dim), jnp.float32)
        log_decay = jnp.zeros((8, head_dim), jnp.float32)
        for j in range(narrow_count):
            fade = in1[j, h, part_rows:, :]
            total = jnp.exp(fade[0:1, :]) * total + in1[j, h, 0:part_rows, :]
            log_decay = log_decay + fade
        out2[h, 0:part_rows, :] = total
        out2[h, part_rows:, :] = log_decay

    @pl.loop(1, wide_count)
    def _(k):
        peer = lax.rem(me + k, wide_count)
        swap2(peer, me).start()

    in2[me] = out2[...]

    @pl.when(is_first)
    def _():
        prev_key[...] = jnp.zeros_like(prev_key)
        prev_value[...] = jnp.zeros_like(prev_value)

    @pl.when(jnp.logical_not(is_first))
    def _():
        pass_on(0).wait_recv()
        pass_on(1).wait_recv()

    no_earlier = jnp.where(is_first, 1, 0)
    reach = causal | (jnp.full((tok_count, tok_count), 1, jnp.int32) * no_earlier == 0)
    for h in range(kv_heads):
        lanes = slice(h * head_dim, (h + 1) * head_dim)
        cum_col, cum_row = sums[h]
        fading = jnp.where(causal, jnp.exp(jnp.where(causal, cum_col - cum_row, 0.0)), 0.0)

        @pl.loop(0, group)
        def _(g):
            at = pl.ds(pl.multiple_of((h * group + g) * head_dim, head_dim), head_dim)
            q = query_ref[:, at]
            own = dot_t(q, key_ref[:, lanes]) * scale
            older = dot_t(q, prev_key[:, lanes]) * scale
            linear[:, at] = dot_split(own * fading, value_ref[:, lanes])
            score = jnp.where(reach, jnp.where(causal, own, older), -jnp.inf)
            expo = jnp.exp(score - jnp.max(score, axis=1, keepdims=True))
            probs = expo / jnp.sum(expo, axis=1, keepdims=True)
            window[:, at] = dot32(
                jnp.where(causal, probs, 0.0).astype(jnp.bfloat16), value_ref[:, lanes]
            ) + dot32(jnp.where(causal, 0.0, probs).astype(jnp.bfloat16), prev_value[:, lanes])

    @pl.loop(1, wide_count)
    def _(k):
        peer = lax.rem(me + k, wide_count)
        swap2(peer, peer).wait_recv()

    for h in range(kv_heads):
        def carry(w, held):
            fresh = jnp.exp(in2[w, h, part_rows : part_rows + 1, :]) * held
            return fresh + in2[w, h, 0:part_rows, :]

        held = lax.fori_loop(0, me, carry, jnp.zeros((part_rows, head_dim), jnp.float32))
        for j in range(narrow_count):
            out3[j, h] = held
            held = jnp.exp(in1[j, h, part_rows : part_rows + 1, :]) * held
            held = held + in1[j, h, 0:part_rows, :]
    for peer in near:
        swap3(peer, here).start()
    in3[here] = out3[here]
    for peer in near:
        swap3(peer, peer).wait_recv()

    def outgoing(c, peer):
        return pltpu.make_async_remote_copy(
            src_ref=send.at[c, peer], dst_ref=recv.at[c, me], send_sem=send_sem.at[c, peer],
            recv_sem=recv_sem.at[c, me], device_id={"wide": peer}, device_id_type=MESH,
        )

    def incoming(c, peer):
        return pltpu.make_async_remote_copy(
            src_ref=send.at[c, peer], dst_ref=recv.at[c, peer], send_sem=send_sem.at[c, peer],
            recv_sem=recv_sem.at[c, peer], device_id={"wide": peer}, device_id_type=MESH,
        )

    def homeward(c, peer, mine):
        return pltpu.make_async_remote_copy(
            src_ref=back.at[c, peer], dst_ref=returned.at[c, mine], send_sem=send_sem2.at[c, peer],
            recv_sem=recv_sem2.at[c, mine], device_id={"wide": peer}, device_id_type=MESH,
        )

    for h in range(kv_heads):
        for j in range(narrow_count):
            high, low = split(in3[j, h])
            state_hi[h, j * part_rows : (j + 1) * part_rows, :] = high
            state_lo[h, j * part_rows : (j + 1) * part_rows, :] = low
        grown = jnp.exp(sums[h][0])

        @pl.loop(0, group)
        def _(g):
            at = pl.ds(pl.multiple_of((h * group + g) * head_dim, head_dim), head_dim)
            q = query_ref[:, at]
            heads = linear[:, at] + (dot32(q, state_hi[h]) + dot32(q, state_lo[h])) * grown
            square = jnp.mean(heads * heads, axis=1, keepdims=True)
            normed = heads / jnp.sqrt(square + 1e-06) * gain_ref[0:1, at]
            attn_ref[:, at] = (normed + window[:, at]).astype(jnp.bfloat16)

        part = slice(h * columns_in, (h + 1) * columns_in)

        @pl.loop(1, wide_count)
        def _(k):
            peer = lax.rem(me + k, wide_count)
            send[h, peer] = dot32(pick[peer], attn_ref[:, part]).astype(jnp.bfloat16)
            outgoing(h, peer).start()

        recv[h, me] = dot32(pick[me], attn_ref[:, part]).astype(jnp.bfloat16)

    chunks = hidden.shape[1] // chunk
    for c in range(parts_in):

        @pl.loop(1, wide_count)
        def _(k):
            peer = lax.rem(me + k, wide_count)
            incoming(c, peer).wait_recv()

        if c == 0:
            for e in range(local_experts):
                up_copy(e).wait()

        @pl.loop(0, local_experts * chunks)
        def _(step):
            e = step // chunks
            at = pl.ds(pl.multiple_of((step % chunks) * chunk, chunk), chunk)
            if local_experts > 1:
                arrived = recv[c].reshape(slots, columns_in)
                token_rows = dot32(order_ref[e, at, :], arrived).astype(jnp.bfloat16)
            else:
                held = pl.ds((step % chunks) * (chunk // rows), chunk // rows)
                token_rows = recv[c, held].reshape(chunk, columns_in)
            summed = dot32(token_rows, up[e, c * columns_in : (c + 1) * columns_in, :])
            if c > 0:
                summed = summed + hidden_sum[e, at, :]
            if c < parts_in - 1:
                hidden_sum[e, at, :] = summed
            else:
                summed = summed * (1.0 / (1.0 + jnp.exp(-summed)))
                hidden[e, at, :] = summed.astype(jnp.bfloat16)

    for e in range(local_experts):
        down_copy(e).wait()
    for c in range(parts_out):
        part = slice(c * columns_out, (c + 1) * columns_out)

        @pl.loop(0, local_experts * chunks)
        def _(step):
            e = step // chunks
            at = pl.ds(pl.multiple_of((step % chunks) * chunk, chunk), chunk)
            result[c, e, at, :] = dot32(hidden[e, at, :], down[e, :, part]).astype(jnp.bfloat16)

        def rows_for(peer):
            if local_experts > 1:
                flat = result[c].reshape(local_experts * hidden.shape[1], columns_out)
                return dot32(back_ref[peer], flat).astype(jnp.bfloat16)
            return result[c, 0, pl.ds(pl.multiple_of(peer * rows, rows), rows), :]

        @pl.loop(1, wide_count)
        def _(k):
            peer = lax.rem(me + k, wide_count)
            back[c, peer] = rows_for(peer)
            homeward(c, peer, me).start()

        returned[c, me] = rows_for(me)

    for c in range(parts_out):
        part = slice(c * columns_out, (c + 1) * columns_out)

        @pl.loop(1, wide_count)
        def _(k):
            peer = lax.rem(me + k, wide_count)
            homeward(c, peer, peer).wait_recv()

        block = returned[c].reshape(slots, columns_out)
        moe = dot32(gates_hi[...], block) + dot32(gates_lo[...], block)
        out_ref[:, part] = (attn_ref[:, part].astype(jnp.float32) + moe).astype(jnp.bfloat16)

    for peer in near:
        swap1(peer, here).wait_send()
        swap3(peer, here).wait_send()

    @pl.when(jnp.logical_not(is_last))
    def _():
        pass_on(0).wait_send()
        pass_on(1).wait_send()

    @pl.loop(1, wide_count)
    def _(k):
        peer = lax.rem(me + k, wide_count)
        swap2(peer, me).wait_send()
        for c in range(parts_in):
            outgoing(c, peer).wait_send()
        for c in range(parts_out):
            homeward(c, peer, me).wait_send()


def per_device(
    queries, key_tensor, value_tensor, decay_logarithm, lin_gain, routes, route_weight, w_up, w_down
):
    wide_count = lax.axis_size("wide")
    narrow_count = lax.axis_size("narrow")
    tok_count, width = queries.shape
    kv_heads = decay_logarithm.shape[0]
    head_dim = key_tensor.shape[1] // kv_heads
    part_rows = head_dim // narrow_count
    units = w_up.shape[1]
    hidden_width = min(units, FF)
    local_experts = units // hidden_width
    blocks_each = hidden_width * QUART // FF
    rows = -(-local_experts * MOST // 16) * 16
    slots = wide_count * rows
    expert, rank = slot_tables(wide_count, local_experts, blocks_each, rows)
    slot_row = np.stack([expert, rank])
    if local_experts > 1:
        order = expert_order(wide_count, local_experts, rows)
        result_rows = wide_count * MOST
        flat = order.reshape(local_experts * result_rows, slots)
        order_back = flat.T.reshape(wide_count, rows, local_experts * result_rows)
    else:
        order = np.zeros((1, 16, 128), np.float32)
        order_back = order
        result_rows = slots
    chunk = result_rows if result_rows <= 128 else 128
    parts_in, parts_out = kv_heads, 4
    bf = jnp.bfloat16
    vmem = pl.BlockSpec(memory_space=pltpu.VMEM)
    hbm = pl.BlockSpec(memory_space=pltpu.HBM)
    dma = pltpu.SemaphoreType.DMA
    return pl.pallas_call(
        functools.partial(layer_kernel, wide_count, narrow_count, local_experts, chunk),
        out_shape=jax.ShapeDtypeStruct((tok_count, width), bf),
        in_specs=[vmem] * 13 + [hbm] * 2,
        out_specs=vmem,
        scratch_shapes=[
            pltpu.VMEM(key_tensor.shape, bf),
            pltpu.VMEM(value_tensor.shape, bf),
            pltpu.VMEM((narrow_count, kv_heads, part_rows + 8, head_dim), jnp.float32),
            pltpu.VMEM((narrow_count, kv_heads, part_rows + 8, head_dim), jnp.float32),
            pltpu.VMEM((kv_heads, part_rows + 8, head_dim), jnp.float32),
            pltpu.VMEM((wide_count, kv_heads, part_rows + 8, head_dim), jnp.float32),
            pltpu.VMEM((narrow_count, kv_heads, part_rows, head_dim), jnp.float32),
            pltpu.VMEM((narrow_count, kv_heads, part_rows, head_dim), jnp.float32),
            pltpu.VMEM((kv_heads, head_dim, head_dim), bf),
            pltpu.VMEM((kv_heads, head_dim, head_dim), bf),
            pltpu.VMEM((tok_count, width), jnp.float32),
            pltpu.VMEM((tok_count, width), jnp.float32),
            pltpu.VMEM((tok_count, width), bf),
            pltpu.VMEM((local_experts, width, hidden_width), bf),
            pltpu.VMEM((local_experts, hidden_width, width), bf),
            pltpu.VMEM((wide_count, rows, tok_count), bf),
            pltpu.VMEM((parts_in, wide_count, rows, width // parts_in), bf),
            pltpu.VMEM((parts_in, wide_count, rows, width // parts_in), bf),
            pltpu.VMEM((local_experts, result_rows, hidden_width), jnp.float32),
            pltpu.VMEM((local_experts, result_rows, hidden_width), bf),
            pltpu.VMEM((parts_out, local_experts, result_rows, width // parts_out), bf),
            pltpu.VMEM((parts_out, wide_count, rows, width // parts_out), bf),
            pltpu.VMEM((parts_out, wide_count, rows, width // parts_out), bf),
            pltpu.VMEM((tok_count, slots), bf),
            pltpu.VMEM((tok_count, slots), bf),
            dma((2,)),
            dma((2,)),
            dma((narrow_count,)),
            dma((narrow_count,)),
            dma((wide_count,)),
            dma((wide_count,)),
            dma((narrow_count,)),
            dma((narrow_count,)),
            dma((local_experts,)),
            dma((local_experts,)),
            dma((parts_in, wide_count)),
            dma((parts_in, wide_count)),
            dma((parts_out, wide_count)),
            dma((parts_out, wide_count)),
        ],
        compiler_params=pltpu.CompilerParams(
            collective_id=0, has_side_effects=True, vmem_limit_bytes=62 * 1024 * 1024
        ),
        name="layer",
    )(
        queries, key_tensor, value_tensor, decay_logarithm, decay_logarithm.T, lin_gain.reshape(1, -1),
        routes, routes.T, route_weight, jnp.asarray(slot_row), jnp.asarray(slot_row.T),
        jnp.asarray(order, bf), jnp.asarray(order_back, bf), w_up, w_down,
    )


def solution(mesh):
    in_specs = (
        P(("wide", "narrow"), None),
        P(("wide", "narrow"), None),
        P(("wide", "narrow"), None),
        P(None, ("wide", "narrow")),
        P(),
        P(("wide", "narrow"), None),
        P(("wide", "narrow"), None),
        P(None, "wide"),
        P("wide", None),
    )
    out_specs = P(("wide", "narrow"), None)
    return jax.shard_map(
        per_device, mesh=mesh, in_specs=in_specs, out_specs=out_specs, check_vma=False
    )
```

```python
import functools

import jax
import jax.numpy as jnp
import numpy as np
from jax import lax
from jax.experimental import pallas as pl
from jax.experimental.pallas import tpu as pltpu
from jax.sharding import PartitionSpec as P

FF = 1408
EXPERTS = 32
TOP = 2
QUART = 4
WINDOW_KEYS = 128
MOST = 12
MESH = pl.DeviceIdType.MESH


def dot32(a, b):
    return jnp.dot(a, b, preferred_element_type=jnp.float32)


def slot_tables(wide_count, local_experts, blocks_each, rows):
    expert = np.full((wide_count, rows), -1, np.int32)
    rank = np.full((wide_count, rows), -1, np.int32)
    for d in range(wide_count):
        for e in range(local_experts):
            block = (d * local_experts + e) * blocks_each
            expert[d, e * MOST : (e + 1) * MOST] = block // QUART
            rank[d, e * MOST : (e + 1) * MOST] = np.arange(MOST)
    return expert.reshape(-1), rank.reshape(-1)


def expert_order(wide_count, local_experts, rows):
    order = np.zeros((local_experts, wide_count * MOST, wide_count * rows), np.float32)
    for e in range(local_experts):
        for d in range(wide_count):
            for m in range(MOST):
                order[e, d * MOST + m, d * rows + e * MOST + m] = 1
    return order


def split(x):
    high = x.astype(jnp.bfloat16)
    return high, (x - high.astype(jnp.float32)).astype(jnp.bfloat16)


def dot_split(a, b):
    high, low = split(a)
    return dot32(high, b) + dot32(low, b)


def dot_t(a, b):
    return lax.dot_general(a, b, (((1,), (1,)), ((), ())), preferred_element_type=jnp.float32)


def layer_kernel(wide_count, narrow_count, local_experts, chunk, *refs):
    (
        query_ref, key_ref, value_ref, decay_ref, gain_ref,
        routes_t_ref, gate_t_ref, slot_row_ref, slot_col_ref, order_ref, back_ref,
        up_hbm, down_hbm, out_ref,
        prev_key, prev_value, out1, in1, out2, in2, out3, in3, state_hi, state_lo, linear, window,
        attn_ref,
        up, down, pick, send, recv, hidden_sum, hidden, result, back, returned, gates_hi, gates_lo,
        kv_send, kv_recv, s1, r1, s2, r2, s3, r3,
        up_sem, down_sem, send_sem, recv_sem, send_sem2, recv_sem2,
    ) = refs
    me = lax.axis_index("wide")
    here = lax.axis_index("narrow")
    hidden_width = up.shape[2]
    tok_count, width = query_ref.shape
    kv_heads = decay_ref.shape[0]
    head_dim = key_ref.shape[1] // kv_heads
    group = width // (kv_heads * head_dim)
    part_rows = head_dim // narrow_count
    scale = head_dim ** (-0.5)
    parts_in, _, rows, columns_in = send.shape
    parts_out, _, _, columns_out = back.shape
    slots = wide_count * rows
    is_first = (me == 0) & (here == 0)
    is_last = (me == wide_count - 1) & (here == narrow_count - 1)
    from_before = (here == 0) & (me > 0)
    to_next = (here == narrow_count - 1) & (me < wide_count - 1)

    def up_copy(e):
        cols = slice(e * hidden_width, (e + 1) * hidden_width)
        src = up_hbm if local_experts == 1 else up_hbm.at[:, cols]
        return pltpu.make_async_copy(src, up.at[e], up_sem.at[e])

    def down_copy(e):
        src = down_hbm.at[e * hidden_width : (e + 1) * hidden_width, :]
        return pltpu.make_async_copy(src, down.at[e], down_sem.at[e])

    barrier = pltpu.get_barrier_semaphore()

    @pl.loop(1, wide_count)
    def _(k):
        peer = lax.rem(me + k, wide_count)
        pl.semaphore_signal(barrier, inc=1, device_id={"wide": peer}, device_id_type=MESH)

    for k in range(1, narrow_count):
        peer = lax.rem(here + k, narrow_count)
        pl.semaphore_signal(barrier, inc=1, device_id={"narrow": peer}, device_id_type=MESH)

    @pl.when(from_before)
    def _():
        target = {"wide": me - 1, "narrow": narrow_count - 1}
        pl.semaphore_signal(barrier, inc=1, device_id=target, device_id_type=MESH)

    @pl.when(to_next)
    def _():
        target = {"wide": me + 1, "narrow": 0}
        pl.semaphore_signal(barrier, inc=1, device_id=target, device_id_type=MESH)

    for e in range(local_experts):
        up_copy(e).start()
    for e in range(local_experts):
        down_copy(e).start()

    at_row = lax.broadcasted_iota(jnp.int32, (tok_count, tok_count), 0)
    at_col = lax.broadcasted_iota(jnp.int32, (tok_count, tok_count), 1)
    causal = at_col <= at_row
    same = at_col == at_row

    def upright(row):
        return jnp.sum(jnp.where(same, row, jnp.zeros_like(row)), axis=1, keepdims=True)

    sums = []
    for h in range(kv_heads):
        decay_row = decay_ref[h : h + 1, :]
        decay_col = upright(decay_row)
        cum_col = jnp.sum(jnp.where(causal, decay_row, 0.0), axis=1, keepdims=True)
        cum_row = jnp.sum(jnp.where(at_row <= at_col, decay_col, 0.0), axis=0, keepdims=True)
        rest = jnp.sum(jnp.where(at_col > at_row, decay_row, 0.0), axis=1, keepdims=True)
        total = jnp.sum(decay_row, axis=1, keepdims=True)
        sums.append((cum_col, cum_row))
        lanes = slice(h * head_dim, (h + 1) * head_dim)
        faded = key_ref[:, lanes].astype(jnp.float32) * (scale * jnp.exp(rest))
        state = dot_split(faded.T, value_ref[:, lanes])
        for j in range(narrow_count):
            out1[j, h, 0:part_rows, :] = state[j * part_rows : (j + 1) * part_rows, :]
            out1[j, h, part_rows:, :] = jnp.broadcast_to(total, (8, head_dim))

    extra = from_before.astype(jnp.int32) + to_next.astype(jnp.int32)
    pl.semaphore_wait(barrier, wide_count - 1 + narrow_count - 1 + extra)

    next_here = lax.rem(here + 1, narrow_count)
    next_wide = lax.rem(me + to_next.astype(jnp.int32), wide_count)

    def pass_on(which):
        src, dst = ((key_ref, prev_key), (value_ref, prev_value))[which]
        return pltpu.make_async_remote_copy(
            src_ref=src, dst_ref=dst, send_sem=kv_send.at[which], recv_sem=kv_recv.at[which],
            device_id={"wide": next_wide, "narrow": next_here}, device_id_type=MESH,
        )

    def swap1(peer, slot):
        return pltpu.make_async_remote_copy(
            src_ref=out1.at[peer], dst_ref=in1.at[slot], send_sem=s1.at[peer],
            recv_sem=r1.at[slot], device_id={"narrow": peer}, device_id_type=MESH,
        )

    def swap2(peer, slot):
        return pltpu.make_async_remote_copy(
            src_ref=out2, dst_ref=in2.at[slot], send_sem=s2.at[peer],
            recv_sem=r2.at[slot], device_id={"wide": peer}, device_id_type=MESH,
        )

    def swap3(peer, slot):
        return pltpu.make_async_remote_copy(
            src_ref=out3.at[peer], dst_ref=in3.at[slot], send_sem=s3.at[peer],
            recv_sem=r3.at[slot], device_id={"narrow": peer}, device_id_type=MESH,
        )

    near = [lax.rem(here + k, narrow_count) for k in range(1, narrow_count)]
    for peer in near:
        swap1(peer, here).start()

    @pl.when(jnp.logical_not(is_last))
    def _():
        pass_on(0).start()
        pass_on(1).start()

    in1[here] = out1[here]

    before = (
        lax.broadcasted_iota(jnp.int32, (tok_count, tok_count), 0)
        < lax.broadcasted_iota(jnp.int32, (tok_count, tok_count), 1)
    ).astype(jnp.bfloat16)
    after = (
        lax.broadcasted_iota(jnp.int32, (tok_count, tok_count), 0)
        > lax.broadcasted_iota(jnp.int32, (tok_count, tok_count), 1)
    ).astype(jnp.bfloat16)
    expert_col = slot_col_ref[:, 0:1]
    rank_col = slot_col_ref[:, 1:2]
    named_t = (routes_t_ref[0:1, :] == expert_col) | (routes_t_ref[1:2, :] == expert_col)
    rank_t = dot32(named_t.astype(jnp.bfloat16), before)
    picked_t = named_t & (rank_t == rank_col.astype(jnp.float32))
    pick[...] = picked_t.astype(jnp.bfloat16).reshape(pick.shape)

    expert_row = slot_row_ref[0:1, :]
    rank_row = slot_row_ref[1:2, :]
    named_by = routes_t_ref[...].astype(jnp.float32)
    first = upright(named_by[0:1, :]) == expert_row.astype(jnp.float32)
    second = upright(named_by[1:2, :]) == expert_row.astype(jnp.float32)
    rank = dot32(after, (first | second).astype(jnp.bfloat16))
    gate = jnp.where(first, upright(gate_t_ref[0:1, :]), 0.0)
    gate = gate + jnp.where(second, upright(gate_t_ref[1:2, :]), 0.0)
    gate = jnp.where(rank == rank_row.astype(jnp.float32), gate, 0.0)
    high = gate.astype(jnp.bfloat16)
    gates_hi[...] = high
    gates_lo[...] = (gate - high.astype(jnp.float32)).astype(jnp.bfloat16)

    for peer in near:
        swap1(peer, peer).wait_recv()
    for h in range(kv_heads):
        total = jnp.zeros((part_rows, head_dim), jnp.float32)
        log_decay = jnp.zeros((8, head_dim), jnp.float32)
        for j in range(narrow_count):
            fade = in1[j, h, part_rows:, :]
            total = jnp.exp(fade[0:1, :]) * total + in1[j, h, 0:part_rows, :]
            log_decay = log_decay + fade
        out2[h, 0:part_rows, :] = total
        out2[h, part_rows:, :] = log_decay

    @pl.loop(1, wide_count)
    def _(k):
        peer = lax.rem(me + k, wide_count)
        swap2(peer, me).start()

    in2[me] = out2[...]

    @pl.when(is_first)
    def _():
        prev_key[...] = jnp.zeros_like(prev_key)
        prev_value[...] = jnp.zeros_like(prev_value)

    @pl.when(jnp.logical_not(is_first))
    def _():
        pass_on(0).wait_recv()
        pass_on(1).wait_recv()

    no_earlier = jnp.where(is_first, 1, 0)
    reach = causal | (jnp.full((tok_count, tok_count), 1, jnp.int32) * no_earlier == 0)
    for h in range(kv_heads):
        lanes = slice(h * head_dim, (h + 1) * head_dim)
        cum_col, cum_row = sums[h]
        fading = jnp.where(causal, jnp.exp(jnp.where(causal, cum_col - cum_row, 0.0)), 0.0)

        @pl.loop(0, group)
        def _(g):
            at = pl.ds(pl.multiple_of((h * group + g) * head_dim, head_dim), head_dim)
            q = query_ref[:, at]
            own = dot_t(q, key_ref[:, lanes]) * scale
            older = dot_t(q, prev_key[:, lanes]) * scale
            linear[:, at] = dot_split(own * fading, value_ref[:, lanes])
            score = jnp.where(reach, jnp.where(causal, own, older), -jnp.inf)
            expo = jnp.exp(score - jnp.max(score, axis=1, keepdims=True))
            probs = expo / jnp.sum(expo, axis=1, keepdims=True)
            window[:, at] = dot32(
                jnp.where(causal, probs, 0.0).astype(jnp.bfloat16), value_ref[:, lanes]
            ) + dot32(jnp.where(causal, 0.0, probs).astype(jnp.bfloat16), prev_value[:, lanes])

    @pl.loop(1, wide_count)
    def _(k):
        peer = lax.rem(me + k, wide_count)
        swap2(peer, peer).wait_recv()

    for h in range(kv_heads):
        def carry(w, held):
            fresh = jnp.exp(in2[w, h, part_rows : part_rows + 1, :]) * held
            return fresh + in2[w, h, 0:part_rows, :]

        held = lax.fori_loop(0, me, carry, jnp.zeros((part_rows, head_dim), jnp.float32))
        for j in range(narrow_count):
            out3[j, h] = held
            held = jnp.exp(in1[j, h, part_rows : part_rows + 1, :]) * held
            held = held + in1[j, h, 0:part_rows, :]
    for peer in near:
        swap3(peer, here).start()
    in3[here] = out3[here]
    for peer in near:
        swap3(peer, peer).wait_recv()

    def outgoing(c, peer):
        return pltpu.make_async_remote_copy(
            src_ref=send.at[c, peer], dst_ref=recv.at[c, me], send_sem=send_sem.at[c, peer],
            recv_sem=recv_sem.at[c, me], device_id={"wide": peer}, device_id_type=MESH,
        )

    def incoming(c, peer):
        return pltpu.make_async_remote_copy(
            src_ref=send.at[c, peer], dst_ref=recv.at[c, peer], send_sem=send_sem.at[c, peer],
            recv_sem=recv_sem.at[c, peer], device_id={"wide": peer}, device_id_type=MESH,
        )

    def homeward(c, peer, mine):
        return pltpu.make_async_remote_copy(
            src_ref=back.at[c, peer], dst_ref=returned.at[c, mine], send_sem=send_sem2.at[c, peer],
            recv_sem=recv_sem2.at[c, mine], device_id={"wide": peer}, device_id_type=MESH,
        )

    for h in range(kv_heads):
        for j in range(narrow_count):
            high, low = split(in3[j, h])
            state_hi[h, j * part_rows : (j + 1) * part_rows, :] = high
            state_lo[h, j * part_rows : (j + 1) * part_rows, :] = low
        grown = jnp.exp(sums[h][0])

        @pl.loop(0, group)
        def _(g):
            at = pl.ds(pl.multiple_of((h * group + g) * head_dim, head_dim), head_dim)
            q = query_ref[:, at]
            heads = linear[:, at] + (dot32(q, state_hi[h]) + dot32(q, state_lo[h])) * grown
            square = jnp.mean(heads * heads, axis=1, keepdims=True)
            normed = heads / jnp.sqrt(square + 1e-06) * gain_ref[0:1, at]
            attn_ref[:, at] = (normed + window[:, at]).astype(jnp.bfloat16)

        part = slice(h * columns_in, (h + 1) * columns_in)

        @pl.loop(1, wide_count)
        def _(k):
            peer = lax.rem(me + k, wide_count)
            send[h, peer] = dot32(pick[peer], attn_ref[:, part]).astype(jnp.bfloat16)
            outgoing(h, peer).start()

        recv[h, me] = dot32(pick[me], attn_ref[:, part]).astype(jnp.bfloat16)

    chunks = hidden.shape[1] // chunk
    for c in range(parts_in):

        @pl.loop(1, wide_count)
        def _(k):
            peer = lax.rem(me + k, wide_count)
            incoming(c, peer).wait_recv()

        if c == 0:
            for e in range(local_experts):
                up_copy(e).wait()

        @pl.loop(0, local_experts * chunks)
        def _(step):
            e = step // chunks
            at = pl.ds(pl.multiple_of((step % chunks) * chunk, chunk), chunk)
            if local_experts > 1:
                arrived = recv[c].reshape(slots, columns_in)
                token_rows = dot32(order_ref[e, at, :], arrived).astype(jnp.bfloat16)
            else:
                held = pl.ds((step % chunks) * (chunk // rows), chunk // rows)
                token_rows = recv[c, held].reshape(chunk, columns_in)
            summed = dot32(token_rows, up[e, c * columns_in : (c + 1) * columns_in, :])
            if c > 0:
                summed = summed + hidden_sum[e, at, :]
            if c < parts_in - 1:
                hidden_sum[e, at, :] = summed
            else:
                summed = summed * (1.0 / (1.0 + jnp.exp(-summed)))
                hidden[e, at, :] = summed.astype(jnp.bfloat16)

    for e in range(local_experts):
        down_copy(e).wait()
    for c in range(parts_out):
        part = slice(c * columns_out, (c + 1) * columns_out)

        @pl.loop(0, local_experts * chunks)
        def _(step):
            e = step // chunks
            at = pl.ds(pl.multiple_of((step % chunks) * chunk, chunk), chunk)
            result[c, e, at, :] = dot32(hidden[e, at, :], down[e, :, part]).astype(jnp.bfloat16)

        def rows_for(peer):
            if local_experts > 1:
                flat = result[c].reshape(local_experts * hidden.shape[1], columns_out)
                return dot32(back_ref[peer], flat).astype(jnp.bfloat16)
            return result[c, 0, pl.ds(pl.multiple_of(peer * rows, rows), rows), :]

        @pl.loop(1, wide_count)
        def _(k):
            peer = lax.rem(me + k, wide_count)
            back[c, peer] = rows_for(peer)
            homeward(c, peer, me).start()

        returned[c, me] = rows_for(me)

    for c in range(parts_out):
        part = slice(c * columns_out, (c + 1) * columns_out)

        @pl.loop(1, wide_count)
        def _(k):
            peer = lax.rem(me + k, wide_count)
            homeward(c, peer, peer).wait_recv()

        block = returned[c].reshape(slots, columns_out)
        moe = dot32(gates_hi[...], block) + dot32(gates_lo[...], block)
        out_ref[:, part] = (attn_ref[:, part].astype(jnp.float32) + moe).astype(jnp.bfloat16)

    for peer in near:
        swap1(peer, here).wait_send()
        swap3(peer, here).wait_send()

    @pl.when(jnp.logical_not(is_last))
    def _():
        pass_on(0).wait_send()
        pass_on(1).wait_send()

    @pl.loop(1, wide_count)
    def _(k):
        peer = lax.rem(me + k, wide_count)
        swap2(peer, me).wait_send()
        for c in range(parts_in):
            outgoing(c, peer).wait_send()
        for c in range(parts_out):
            homeward(c, peer, me).wait_send()


def per_device(
    queries, key_tensor, value_tensor, decay_logarithm, lin_gain, routes, route_weight, w_up, w_down
):
    wide_count = lax.axis_size("wide")
    narrow_count = lax.axis_size("narrow")
    tok_count, width = queries.shape
    kv_heads = decay_logarithm.shape[0]
    head_dim = key_tensor.shape[1] // kv_heads
    part_rows = head_dim // narrow_count
    units = w_up.shape[1]
    hidden_width = min(units, FF)
    local_experts = units // hidden_width
    blocks_each = hidden_width * QUART // FF
    rows = -(-local_experts * MOST // 16) * 16
    slots = wide_count * rows
    expert, rank = slot_tables(wide_count, local_experts, blocks_each, rows)
    slot_row = np.stack([expert, rank])
    if local_experts > 1:
        order = expert_order(wide_count, local_experts, rows)
        result_rows = wide_count * MOST
        flat = order.reshape(local_experts * result_rows, slots)
        order_back = flat.T.reshape(wide_count, rows, local_experts * result_rows)
    else:
        order = np.zeros((1, 16, 128), np.float32)
        order_back = order
        result_rows = slots
    chunk = result_rows if result_rows <= 128 else 128
    parts_in, parts_out = kv_heads, 4
    bf = jnp.bfloat16
    vmem = pl.BlockSpec(memory_space=pltpu.VMEM)
    hbm = pl.BlockSpec(memory_space=pltpu.HBM)
    dma = pltpu.SemaphoreType.DMA
    return pl.pallas_call(
        functools.partial(layer_kernel, wide_count, narrow_count, local_experts, chunk),
        out_shape=jax.ShapeDtypeStruct((tok_count, width), bf),
        in_specs=[vmem] * 11 + [hbm] * 2,
        out_specs=vmem,
        scratch_shapes=[
            pltpu.VMEM(key_tensor.shape, bf),
            pltpu.VMEM(value_tensor.shape, bf),
            pltpu.VMEM((narrow_count, kv_heads, part_rows + 8, head_dim), jnp.float32),
            pltpu.VMEM((narrow_count, kv_heads, part_rows + 8, head_dim), jnp.float32),
            pltpu.VMEM((kv_heads, part_rows + 8, head_dim), jnp.float32),
            pltpu.VMEM((wide_count, kv_heads, part_rows + 8, head_dim), jnp.float32),
            pltpu.VMEM((narrow_count, kv_heads, part_rows, head_dim), jnp.float32),
            pltpu.VMEM((narrow_count, kv_heads, part_rows, head_dim), jnp.float32),
            pltpu.VMEM((kv_heads, head_dim, head_dim), bf),
            pltpu.VMEM((kv_heads, head_dim, head_dim), bf),
            pltpu.VMEM((tok_count, width), jnp.float32),
            pltpu.VMEM((tok_count, width), jnp.float32),
            pltpu.VMEM((tok_count, width), bf),
            pltpu.VMEM((local_experts, width, hidden_width), bf),
            pltpu.VMEM((local_experts, hidden_width, width), bf),
            pltpu.VMEM((wide_count, rows, tok_count), bf),
            pltpu.VMEM((parts_in, wide_count, rows, width // parts_in), bf),
            pltpu.VMEM((parts_in, wide_count, rows, width // parts_in), bf),
            pltpu.VMEM((local_experts, result_rows, hidden_width), jnp.float32),
            pltpu.VMEM((local_experts, result_rows, hidden_width), bf),
            pltpu.VMEM((parts_out, local_experts, result_rows, width // parts_out), bf),
            pltpu.VMEM((parts_out, wide_count, rows, width // parts_out), bf),
            pltpu.VMEM((parts_out, wide_count, rows, width // parts_out), bf),
            pltpu.VMEM((tok_count, slots), bf),
            pltpu.VMEM((tok_count, slots), bf),
            dma((2,)),
            dma((2,)),
            dma((narrow_count,)),
            dma((narrow_count,)),
            dma((wide_count,)),
            dma((wide_count,)),
            dma((narrow_count,)),
            dma((narrow_count,)),
            dma((local_experts,)),
            dma((local_experts,)),
            dma((parts_in, wide_count)),
            dma((parts_in, wide_count)),
            dma((parts_out, wide_count)),
            dma((parts_out, wide_count)),
        ],
        compiler_params=pltpu.CompilerParams(
            collective_id=0, has_side_effects=True, vmem_limit_bytes=63 * 1024 * 1024
        ),
        name="layer",
    )(
        queries, key_tensor, value_tensor, decay_logarithm, lin_gain.reshape(1, -1),
        routes.T, route_weight.T, jnp.asarray(slot_row), jnp.asarray(slot_row.T),
        jnp.asarray(order, bf), jnp.asarray(order_back, bf), w_up, w_down,
    )


def solution(mesh):
    in_specs = (
        P(("wide", "narrow"), None),
        P(("wide", "narrow"), None),
        P(("wide", "narrow"), None),
        P(None, ("wide", "narrow")),
        P(),
        P(("wide", "narrow"), None),
        P(("wide", "narrow"), None),
        P(None, "wide"),
        P("wide", None),
    )
    out_specs = P(("wide", "narrow"), None)
    return jax.shard_map(
        per_device, mesh=mesh, in_specs=in_specs, out_specs=out_specs, check_vma=False
    )
```
